256 devices in a mesh: snode: 32 (over x, z), col: 8 (over y, core).
Axes of the slice: x: 4, y: 4, z: 8, core: 2. Of those that a mesh axis runs over, the one named last changes fastest.
Arguments:
- rhs: float32 [3, 32768, 256], P(None, ('snode', 'col')), may hold values from -6 to 6
- dinv: bfloat16 [3, 32768, 1024], P(None, ('snode', 'col')), may hold values from -2 to 2, as said below
- loff: bfloat16 [2, 524288, 1024], P(None, ('snode', 'col')), may hold values from -0.046875 to 0.046875
- targets: int32 [2, 4096], P(None, ('snode', 'col')), may hold values from 0 to 31, as said below
Outputs:
- solution: float32 [3, 32768, 256], P(None, ('snode', 'col'))
The draws below stay inside these ranges and needn't reach their ends.
Inputs may be any that keep to these rules, and one draw needn't show every extreme that they name: `targets`: the 16 entries that one device holds for one level are distinct. `dinv`: each block is the inverse of a lower-triangular block: lower triangular, with diagonal entries from 0.5 to 2.
All inputs are finite; a program needn't handle non-finite values.
Results may differ from the reference program's by a relative error of at most 0.025.
Values may be sent and summed in bfloat16 or wider, within the bound.
No kernel may reach another device: no remote copies, remote signals or barrier semaphores. Data moves between devices by JAX's collectives and lax.ppermute only.
A program may use at most 64 MiB of HBM per device.

```python
import math
import jax
import jax.numpy as jnp
from jax import lax

W = 1024
BLK = 128
NRHS = 256
LEVELS = 3
OFF_DEV = 16
TARGETS = 32
NROWS = 32768
NLINKS = 4096
NOFF = 524288
N_SNODE = 32
N_COL = 8


def draw_targets(key, part):
    count = (LEVELS - 1) * NLINKS // OFF_DEV
    keys = jax.random.split(key, count)
    picks = jax.vmap(lambda single_key: jax.random.permutation(single_key, TARGETS)[:OFF_DEV])(keys)
    return picks.reshape(LEVELS - 1, NLINKS).astype(jnp.int32)


def draw_dinv(key, part):
    key_diag, key_off = jax.random.split(jax.random.fold_in(key, 7))
    shape = (LEVELS, NROWS, W)
    row_index = lax.broadcasted_iota(jnp.int32, shape, 1) % W
    col_index = lax.broadcasted_iota(jnp.int32, shape, 2)
    below = 1.5 * jax.random.normal(key_off, shape, jnp.float32) / math.sqrt(W)
    diagonal = jnp.exp(jax.random.uniform(key_diag, shape, jnp.float32, math.log(0.5), math.log(2.0)))
    values = jnp.where(col_index < row_index, below, jnp.where(col_index == row_index, diagonal, 0.0))
    return values.astype(jnp.bfloat16)


def block_levels(stream_key, shape, pieces, low, top_value):
    def one(axis_at, blocks):
        steps = jax.random.uniform(jax.random.fold_in(jax.random.fold_in(stream_key, 6), axis_at), (blocks,), jnp.float32, low / len(pieces), top_value / len(pieces))
        return jnp.repeat(jnp.exp(steps), shape[axis_at] // blocks).reshape((-1,) + (1,) * (len(shape) - axis_at - 1))

    gain = one(*pieces[0])
    for cut in pieces[1:]:
        gain = gain * one(*cut)
    return gain


def noise(own_key, shape, deviation, limit, cuts=(), dtype=jnp.bfloat16):
    array = deviation * jax.random.normal(own_key, shape, jnp.float32)
    if cuts:
        array = array * block_levels(own_key, shape, cuts, -0.22, 0.18)
    return jnp.clip(array, -limit, limit).astype(dtype)


def setup_inputs(seed: int = 0) -> dict:
    key_of = jax.random.split(jax.random.key(seed), 5)
    rhs = noise(key_of[0], (LEVELS, NROWS, NRHS), 1.0, 6.0, ((1, 256),), jnp.float32)
    dinv = draw_dinv(jax.random.fold_in(key_of[4], 71), 0)
    loff = noise(key_of[2], (LEVELS - 1, NOFF, W), (W * OFF_DEV) ** -0.5, 0.046875, ((1, 256),))
    targets = draw_targets(jax.random.fold_in(key_of[4], 71), 0)
    return {"rhs": rhs, "dinv": dinv, "loff": loff, "targets": targets}


def diag_apply(inverse_level, vector_bf, transpose):
    blocks = inverse_level.reshape(N_SNODE, W, W)
    vectors = vector_bf.reshape(N_SNODE, W, NRHS)

    def single(pair):
        matrix, vector = pair
        if transpose:
            return jnp.dot(matrix.T, vector, preferred_element_type=jnp.float32)
        return jnp.dot(matrix, vector, preferred_element_type=jnp.float32)

    return lax.map(single, (blocks, vectors)).reshape(NROWS, NRHS)


def spread(loff_level, links, solved_bf, per_col):
    blocks = loff_level.reshape(N_SNODE, N_COL * OFF_DEV * BLK, W)
    solved = solved_bf.reshape(N_SNODE, W, NRHS)
    dest = links.reshape(N_SNODE, N_COL * OFF_DEV)
    col_index = (jnp.arange(N_COL * OFF_DEV) // OFF_DEV).astype(jnp.int32)

    def advance(running, item):
        blocks_here, solved_here, target = item
        update = jnp.dot(blocks_here, solved_here, preferred_element_type=jnp.float32).astype(jnp.bfloat16)
        update = lax.optimization_barrier(update)
        update = update.astype(jnp.float32).reshape(N_COL * OFF_DEV, BLK, NRHS)
        running = running.at[target // per_col, col_index, target % per_col].add(update)
        return running, None

    initial = jnp.zeros((N_SNODE, N_COL, per_col, BLK, NRHS), jnp.float32)
    running, unused = lax.scan(advance, initial, (blocks, solved, dest))
    return running.reshape(NROWS, NRHS)


def gather_back(loff_level, links, upper_bf, per_col):
    blocks = loff_level.reshape(N_SNODE, N_COL * OFF_DEV * BLK, W)
    upper = upper_bf.reshape(N_SNODE, N_COL, per_col, BLK, NRHS)
    dest = links.reshape(N_SNODE, N_COL, OFF_DEV)
    col_index = lax.broadcasted_iota(jnp.int32, (N_COL, OFF_DEV), 0)

    def single(pair):
        blocks_here, target = pair
        picked = upper[target // per_col, col_index, target % per_col]
        picked = picked.reshape(N_COL * OFF_DEV * BLK, NRHS)
        return jnp.dot(blocks_here.T, picked, preferred_element_type=jnp.float32)

    return lax.map(single, (blocks, dest)).reshape(NROWS, NRHS)


def reference(rhs, dinv, loff, targets):
    per_col = W // BLK // N_COL
    incoming = jnp.zeros((NROWS, NRHS), jnp.float32)
    forward = []
    for level in range(LEVELS):
        resid_bf = (rhs[level] - incoming).astype(jnp.bfloat16)
        solved = diag_apply(dinv[level], resid_bf, False)
        forward.append(solved)
        if level + 1 < LEVELS:
            incoming = spread(loff[level], targets[level], solved.astype(jnp.bfloat16), per_col)
    results = [None] * LEVELS
    upper_bf = None
    for level in reversed(range(LEVELS)):
        reduced = forward[level]
        if level + 1 < LEVELS:
            reduced = reduced - gather_back(loff[level], targets[level], upper_bf, per_col)
        solved = diag_apply(dinv[level], reduced.astype(jnp.bfloat16), True)
        results[level] = solved
        upper_bf = solved.astype(jnp.bfloat16)
    return jnp.stack(results)
```

```python
import functools
import jax
import jax.numpy as jnp
from jax import lax
from jax.experimental import pallas as pl
from jax.experimental.pallas import tpu as pltpu
from jax.sharding import Mesh, PartitionSpec as P

BLK = 128
NX, NZ, NY, NC = 4, 8, 4, 2
NCOL = NY * NC
W = NCOL * BLK
OFF = 16
STEPS = 4
PER = OFF // STEPS
F32, BF16 = jnp.float32, jnp.bfloat16
CHAINS = 1

SMEM = pl.BlockSpec(memory_space=pltpu.SMEM)
VMEM = pl.BlockSpec(memory_space=pltpu.VMEM)
PARAMS = pltpu.CompilerParams(vmem_limit_bytes=32 * 1024 * 1024)


def shape(dims, dtype):
    return jax.ShapeDtypeStruct(dims, dtype)


def take(value, axis, size, shift):
    return lax.ppermute(value, axis, [(i, (i - shift) % size) for i in range(size)])


def give(value, axis, size, shift):
    return lax.ppermute(value, axis, [(i, (i + shift) % size) for i in range(size)])


def gather_col(value):
    rows = [value] + [take(value, "y", NY, d) for d in range(1, NY)]
    return rows + [take(v, "core", NC, 1) for v in rows]


def fill(place, parts, full):
    for i in range(NCOL):
        start = pl.multiple_of(place[i] * BLK, BLK)
        full[pl.ds(start, BLK), :] = parts[i][...]


def own_rows_kernel(place, *refs):
    parts, matrix, out, full = refs[:NCOL], refs[NCOL], refs[NCOL + 1], refs[NCOL + 2]
    fill(place, parts, full)
    out[...] = jnp.dot(matrix[0], full[...], preferred_element_type=F32).astype(BF16)


def own_rows(place, parts, dinv):
    n = parts[0].shape[1]
    return pl.pallas_call(
        own_rows_kernel,
        out_shape=shape((BLK, n), BF16),
        grid=(1,),
        in_specs=[SMEM]
        + [pl.BlockSpec((BLK, n), lambda i: (0, 0))] * NCOL
        + [pl.BlockSpec((1, BLK, W), lambda i: (0, 0, 0))],
        out_specs=pl.BlockSpec((BLK, n), lambda i: (0, 0)),
        scratch_shapes=[pltpu.VMEM((W, n), BF16)],
        compiler_params=PARAMS,
    )(place, *parts, dinv)


def update_kernel(solve, slots, place, *refs):
    parts, refs = refs[:NCOL], refs[NCOL:]
    if solve:
        matrix, refs = refs[0], refs[1:]
    blocks, outs, full_out, full, piece = refs[0], refs[1 : 1 + NX], refs[1 + NX], refs[2 + NX], refs[3 + NX]
    step = pl.program_id(0)

    @pl.when(step == 0)
    def begin():
        for out in outs:
            out[...] = jnp.zeros_like(out)
        fill(place, parts, full)
        if solve:
            full[...] = jnp.dot(matrix[...], full[...], preferred_element_type=F32).astype(BF16)
        full_out[...] = full[...]

    piece[...] = jnp.dot(blocks[0], full[...], preferred_element_type=F32).astype(BF16)
    for k in range(PER):
        slot = slots[step * PER + k]
        along_x = slot // NZ
        start = pl.multiple_of((slot % NZ) * BLK, BLK)
        for d in range(NX):

            @pl.when(along_x == d)
            def put():
                outs[d][pl.ds(start, BLK), :] = piece[k * BLK : (k + 1) * BLK, :]


def update(level, slots, place, parts, matrix, loff):
    n = parts[0].shape[1]
    solve = matrix is not None
    const = lambda i: (0, 0)
    in_specs = [SMEM, SMEM] + [pl.BlockSpec((BLK, n), const)] * NCOL
    args = [slots, place, *parts]
    if solve:
        in_specs.append(pl.BlockSpec((W, W), const))
        args.append(matrix)
    in_specs.append(pl.BlockSpec((1, PER * BLK, W), lambda i: (level, i, 0)))
    args.append(loff)
    *outs, full = pl.pallas_call(
        functools.partial(update_kernel, solve),
        out_shape=[shape((NZ * BLK, n), BF16)] * NX + [shape((W, n), BF16)],
        grid=(STEPS,),
        in_specs=in_specs,
        out_specs=[pl.BlockSpec((NZ * BLK, n), const)] * NX + [pl.BlockSpec((W, n), const)],
        scratch_shapes=[pltpu.VMEM((W, n), BF16), pltpu.VMEM((PER * BLK, n), BF16)],
        compiler_params=PARAMS,
    )(*args)
    return outs, full


def sum_x_kernel(*refs):
    ins, outs = refs[:NX], refs[NX:]
    for z in range(NZ):
        rows = slice(z * BLK, (z + 1) * BLK)
        total = ins[0][rows, :].astype(F32)
        for other in ins[1:]:
            total += other[rows, :].astype(F32)
        outs[z][...] = total.astype(outs[z].dtype)


def sum_x(ins):
    n = ins[0].shape[1]
    return pl.pallas_call(
        sum_x_kernel,
        out_shape=[shape((BLK, n), F32)] + [shape((BLK, n), BF16)] * (NZ - 1),
        in_specs=[VMEM] * NX,
        out_specs=[VMEM] * NZ,
        compiler_params=PARAMS,
    )(*ins)


def route(outs):
    got = [outs[0]] + [give(outs[d], "x", NX, d) for d in range(1, NX)]
    parts = sum_x(got)
    total = parts[0]
    for d in range(1, NZ):
        total = total + give(parts[d], "z", NZ, d).astype(F32)
    return total


def top_kernel(col, place, *refs):
    parts, matrix, out, out_bf, full = refs[:NCOL], *refs[NCOL:]
    fill(place, parts, full)
    forward = jnp.dot(matrix[...], full[...], preferred_element_type=F32)
    mine = matrix[:, pl.ds(pl.multiple_of(col[0] * BLK, BLK), BLK)]
    solved = jnp.dot(forward.T.astype(BF16), mine, preferred_element_type=F32)
    out[...] = solved
    out_bf[...] = solved.astype(BF16)


def top(col, place, parts, matrix):
    n = parts[0].shape[1]
    return pl.pallas_call(
        top_kernel,
        out_shape=[shape((n, BLK), F32), shape((n, BLK), BF16)],
        in_specs=[SMEM, SMEM] + [VMEM] * (NCOL + 1),
        out_specs=[VMEM, VMEM],
        scratch_shapes=[pltpu.VMEM((W, n), BF16)],
        compiler_params=PARAMS,
    )(col, place, *parts, matrix)


def base_kernel(col, full, matrix, out):
    mine = matrix[:, pl.ds(pl.multiple_of(col[0] * BLK, BLK), BLK)]
    out[...] = jnp.dot(full[...].T, mine, preferred_element_type=F32)


def base_term(col, full, matrix):
    n = full.shape[1]
    return pl.pallas_call(
        base_kernel,
        out_shape=shape((n, BLK), F32),
        in_specs=[SMEM, VMEM, VMEM],
        out_specs=VMEM,
        compiler_params=PARAMS,
    )(col, full, matrix)


def fetch(value):
    column = jnp.stack([value] + [take(value, "z", NZ, d) for d in range(1, NZ)])
    return [column] + [take(column, "x", NX, d) for d in range(1, NX)]


def back_kernel(slots, place, *refs):
    upper, matrix, blocks, own, other, picked, total = refs[:NX], *refs[NX:]
    step = pl.program_id(0)
    for k in range(PER):
        slot = slots[step * PER + k]
        along_x, along_z = slot // NZ, slot % NZ
        for d in range(NX):

            @pl.when(along_x == d)
            def pick():
                picked[:, k * BLK : (k + 1) * BLK] = upper[d][along_z]

    term = jnp.dot(picked[...], blocks[0], preferred_element_type=F32)

    @pl.when(step == 0)
    def first():
        total[...] = term

    @pl.when(step > 0)
    def later():
        total[...] += term

    @pl.when(step == STEPS - 1)
    def end():
        total[...] = jnp.dot(total[...].astype(BF16), matrix[...], preferred_element_type=F32)
        for i in range(NY):
            start = pl.multiple_of(place[i] * BLK, BLK)
            own[i] = total[:, pl.ds(start, BLK)]
            start = pl.multiple_of(place[NY + i] * BLK, BLK)
            other[i] = total[:, pl.ds(start, BLK)].astype(BF16)


def back(level, slots, place, upper, matrix, loff):
    n = upper[0].shape[1]
    return pl.pallas_call(
        back_kernel,
        out_shape=[shape((NY, n, BLK), F32), shape((NY, n, BLK), BF16)],
        grid=(STEPS,),
        in_specs=[SMEM, SMEM]
        + [pl.BlockSpec((NZ, n, BLK), lambda i: (0, 0, 0))] * NX
        + [
            pl.BlockSpec((W, W), lambda i: (0, 0)),
            pl.BlockSpec((1, PER * BLK, W), lambda i: (level, i, 0)),
        ],
        out_specs=[pl.BlockSpec((NY, n, BLK), lambda i: (0, 0, 0))] * 2,
        scratch_shapes=[pltpu.VMEM((n, PER * BLK), BF16), pltpu.VMEM((n, W), F32)],
        compiler_params=PARAMS,
    )(slots, place, *upper, matrix, loff)


def sum_core_kernel(own, other, mine, *outs):
    mine[...] = own[0] + other[0].astype(F32)
    for i in range(1, NY):
        outs[i - 1][...] = (own[i] + other[i].astype(F32)).astype(BF16)


def sum_core(own, other):
    n = own.shape[1]
    return pl.pallas_call(
        sum_core_kernel,
        out_shape=[shape((n, BLK), F32)] + [shape((n, BLK), BF16)] * (NY - 1),
        in_specs=[VMEM] * 2,
        out_specs=[VMEM] * NY,
        compiler_params=PARAMS,
    )(own, other)


def reduce_col(own, other):
    parts = sum_core(own, take(other, "core", NC, 1))
    total = parts[0]
    for d in range(1, NY):
        total = total + give(parts[d], "y", NY, d).astype(F32)
    return total


def body(rhs, dinv, loff, targets):
    levels = rhs.shape[0]
    count = rhs.shape[2]
    n = count // CHAINS
    x, z = lax.axis_index("x"), lax.axis_index("z")
    y, core = lax.axis_index("y"), lax.axis_index("core")
    order = jnp.arange(NY, dtype=jnp.int32)
    rows = (y + order) % NY * NC
    place = jnp.concatenate([rows + core, rows + 1 - core]).astype(jnp.int32)
    col = (y * NC + core).reshape(1).astype(jnp.int32)
    slots = (targets // NZ - x) % NX * NZ + (targets % NZ - z) % NZ
    slots = slots.astype(jnp.int32)
    full_d = [None] * levels
    for level in list(range(1, levels)) + [0]:
        full_d[level] = lax.all_gather(dinv[level], ("y", "core"), axis=0, tiled=True)

    chains = []
    for chain in range(CHAINS):
        part = rhs[:, :, chain * n : (chain + 1) * n]
        bases = []
        incoming = None
        for level in range(levels - 1):
            resid = part[level] if level == 0 else part[level] - incoming
            parts = gather_col(resid.astype(BF16))
            if level == 0:
                parts = gather_col(own_rows(place, parts, dinv))
            outs, full = update(level, slots[level], place, parts, full_d[level] if level else None, loff)
            bases.append(base_term(col, full, full_d[level]))
            incoming = route(outs)
        parts = gather_col((part[levels - 1] - incoming).astype(BF16))
        solved, solved_bf = top(col, place, parts, full_d[levels - 1])
        outputs = [None] * levels
        outputs[levels - 1] = solved.T
        for level in reversed(range(levels - 1)):
            upper = fetch(solved_bf)
            own, other = back(level, slots[level], place, upper, full_d[level], loff)
            solved = bases[level] - reduce_col(own, other)
            solved_bf = solved.astype(BF16)
            outputs[level] = solved.T
        chains.append(jnp.stack(outputs))
    return chains[0] if CHAINS == 1 else jnp.concatenate(chains, axis=2)


def solution(mesh):
    grid = Mesh(mesh.devices.reshape(NX, NZ, NY, NC), ("x", "z", "y", "core"))
    split = ("x", "z", "y", "core")
    in_specs = (P(None, split, None), P(None, split, None), P(None, split, None), P(None, split))
    out_specs = P(None, split, None)
    return jax.shard_map(body, mesh=grid, in_specs=in_specs, out_specs=out_specs, check_vma=False)
```

```python
import functools
import jax
import jax.numpy as jnp
from jax import lax
from jax.experimental import pallas as pl
from jax.experimental.pallas import tpu as pltpu
from jax.sharding import Mesh, PartitionSpec as P

BLK = 128
NX, NZ, NY, NC = 4, 8, 4, 2
NCOL = NY * NC
W = NCOL * BLK
OFF = 16
STEPS = 4
PER = OFF // STEPS
F32, BF16 = jnp.float32, jnp.bfloat16
VLIM = 24
HOLD = 50
GROUPS = ((2,), (1, 3), (0,))
EVEN = (2, 0, 6, 4)

SMEM = pl.BlockSpec(memory_space=pltpu.SMEM)
VMEM = pl.BlockSpec(memory_space=pltpu.VMEM)
ANY = pl.BlockSpec(memory_space=pl.ANY)
PARAMS = pltpu.CompilerParams(vmem_limit_bytes=VLIM * 1024 * 1024)


def shape(dims, dtype):
    return jax.ShapeDtypeStruct(dims, dtype)


def take(value, axis, size, shift):
    return lax.ppermute(value, axis, [(i, (i - shift) % size) for i in range(size)])


def give(value, axis, size, shift):
    return lax.ppermute(value, axis, [(i, (i + shift) % size) for i in range(size)])


def gather_col(value):
    rows = [value] + [take(value, "y", NY, d) for d in range(1, NY)]
    return rows + [take(v, "core", NC, 1) for v in rows]


def fill(place, parts, full):
    for i in range(NCOL):
        start = pl.multiple_of(place[i] * BLK, BLK)
        full[pl.ds(start, BLK), :] = parts[i][...]


def own_rows_kernel(place, *refs):
    parts, (matrix, _, out, full) = refs[:NCOL], refs[NCOL:]
    fill(place, parts, full)
    out[...] = jnp.dot(matrix[0], full[...], preferred_element_type=F32).astype(BF16)


def own_rows(place, parts, dinv, after):
    n = parts[0].shape[1]
    return pl.pallas_call(
        own_rows_kernel,
        out_shape=shape((BLK, n), BF16),
        grid=(1,),
        in_specs=[SMEM]
        + [pl.BlockSpec((BLK, n), lambda i: (0, 0))] * NCOL
        + [pl.BlockSpec((1, BLK, W), lambda i: (0, 0, 0)), ANY],
        out_specs=pl.BlockSpec((BLK, n), lambda i: (0, 0)),
        scratch_shapes=[pltpu.VMEM((W, n), BF16)],
        compiler_params=PARAMS,
    )(place, *parts, dinv, after)


def hold_kernel(count, source, *refs):
    outs, sems = refs[:count], refs[count]
    copies = [pltpu.make_async_copy(source.at[i], outs[i], sems.at[i]) for i in range(count)]
    for copy in copies:
        copy.start()
    for copy in copies:
        copy.wait()


def hold(stacked, limit):
    count, dims = stacked.shape[0], stacked.shape[1:]
    return pl.pallas_call(
        functools.partial(hold_kernel, count),
        out_shape=[pltpu.VMEM(dims, stacked.dtype)] * count,
        in_specs=[ANY],
        out_specs=[VMEM] * count,
        scratch_shapes=[pltpu.SemaphoreType.DMA((count,))],
        compiler_params=pltpu.CompilerParams(vmem_limit_bytes=limit * 1024 * 1024),
        cost_estimate=pl.CostEstimate(flops=0, bytes_accessed=2 * stacked.size * 2, transcendentals=0),
    )(stacked)


def forward_table():
    table = [0] * (NX * NZ)
    for g, group in enumerate(GROUPS):
        for i, dx in enumerate(group):
            for j, dz in enumerate(EVEN):
                table[dx * NZ + dz] = (3 * g) * 16 + i * 4 + j
            for kind, odd in enumerate(((3, 1), (7, 5))):
                for j, dz in enumerate(odd):
                    table[dx * NZ + dz] = (3 * g + 1 + kind) * 16 + i * 2 + j
    return table


def backward_table():
    table = [0] * (NX * NZ)
    for g, group in enumerate(GROUPS):
        for i, dx in enumerate(group):
            for j, dz in enumerate(EVEN):
                table[dx * NZ + dz] = dx * 16 + j
            for kind, odd in enumerate(((3, 1), (7, 5))):
                for j, dz in enumerate(odd):
                    table[dx * NZ + dz] = (NX + 2 * g + kind) * 16 + i * 2 + j
    return table


def look_up(table, slots):
    wanted = lax.iota(jnp.int32, len(table))
    values = jnp.array(table, jnp.int32)
    return jnp.sum(jnp.where(slots[..., None] == wanted, values, 0), axis=-1, dtype=jnp.int32)


def update_kernel(solve, count, slots, place, *refs):
    parts, refs = refs[:NCOL], refs[NCOL:]
    if solve:
        matrix, refs = refs[0], refs[1:]
    blocks, outs, refs = refs[0], refs[1 : 1 + count], refs[1 + count :]
    full_out, full, piece = refs
    for out in outs:
        out[...] = jnp.zeros_like(out)
    fill(place, parts, full)
    if solve:
        full[...] = jnp.dot(matrix[...], full[...], preferred_element_type=F32).astype(BF16)
    full_out[...] = full[...]
    for step in range(STEPS):
        rows = slice(step * PER * BLK, (step + 1) * PER * BLK)
        piece[...] = jnp.dot(blocks[rows, :], full[...], preferred_element_type=F32).astype(BF16)
        for k in range(PER):
            slot = slots[step * PER + k]
            which, where = slot // 16, slot % 16
            for d in range(count):

                @pl.when(which == d)
                def put():
                    outs[d][where] = piece[k * BLK : (k + 1) * BLK, :]


def update(slots, place, parts, matrix, held):
    n = parts[0].shape[1]
    solve = matrix is not None
    args = [slots, place, *parts] + ([matrix] if solve else []) + [held]
    outs = [(len(group) * k, BLK, n) for group in GROUPS for k in (4, 2, 2)]
    *outs, full = pl.pallas_call(
        functools.partial(update_kernel, solve, len(outs)),
        out_shape=[shape(dims, BF16) for dims in outs] + [shape((W, n), BF16)],
        in_specs=[SMEM, SMEM] + [VMEM] * (len(args) - 2),
        out_specs=[VMEM] * (len(outs) + 1),
        scratch_shapes=[pltpu.VMEM((W, n), BF16), pltpu.VMEM((PER * BLK, n), BF16)],
        compiler_params=PARAMS,
    )(*args)
    return outs, full


def sum_near_kernel(even, up, down, _, *outs):
    for i, out in enumerate(outs):
        e = [even[4 * i + j].astype(F32) for j in range(4)]
        e[0] = e[0] + up[2 * i].astype(F32)
        e[1] = e[1] + up[2 * i + 1].astype(F32) + down[2 * i].astype(F32)
        e[2] = e[2] + down[2 * i + 1].astype(F32)
        for j in range(4):
            out[j] = e[j].astype(out.dtype)


def sum_near(group, even, up, down, after):
    n = even.shape[2]
    return pl.pallas_call(
        sum_near_kernel,
        out_shape=[shape((4, BLK, n), BF16 if dx else F32) for dx in group],
        in_specs=[VMEM] * 3 + [ANY],
        out_specs=[VMEM] * len(group),
        compiler_params=PARAMS,
    )(even, up, down, after)


def sum_x_kernel(*refs):
    ins, outs = refs[:NX], refs[NX + 1 :]
    for j in range(4):
        total = ins[0][j].astype(F32)
        for other in ins[1:]:
            total += other[j].astype(F32)
        outs[j][...] = total.astype(outs[j].dtype)


def sum_x(ins, after):
    n = ins[0].shape[2]
    return pl.pallas_call(
        sum_x_kernel,
        out_shape=[shape((BLK, n), BF16 if dz else F32) for dz in EVEN],
        in_specs=[VMEM] * NX + [ANY],
        out_specs=[VMEM] * 4,
        compiler_params=PARAMS,
    )(*ins, after)


def route(outs, first, second):
    got = [None] * NX
    for g, group in enumerate(GROUPS):
        even, up, down = outs[3 * g : 3 * g + 3]
        sums = sum_near(group, even, give(up, "z", NZ, 1), give(down, "z", NZ, -1), first)
        for dx, value in zip(group, sums):
            got[dx] = give(value, "x", NX, dx) if dx else value
    parts = sum_x(got, second)
    total = parts[EVEN.index(0)]
    for j, dz in enumerate(EVEN):
        if dz:
            total = total + give(parts[j], "z", NZ, dz).astype(F32)
    return total


def top_kernel(col, place, *refs):
    parts, matrix, out, out_bf, full = refs[:NCOL], *refs[NCOL:]
    fill(place, parts, full)
    forward = jnp.dot(matrix[...], full[...], preferred_element_type=F32)
    mine = matrix[:, pl.ds(pl.multiple_of(col[0] * BLK, BLK), BLK)]
    solved = jnp.dot(forward.T.astype(BF16), mine, preferred_element_type=F32)
    out[...] = solved
    out_bf[...] = solved.astype(BF16)


def top(col, place, parts, matrix):
    n = parts[0].shape[1]
    return pl.pallas_call(
        top_kernel,
        out_shape=[shape((n, BLK), F32), shape((n, BLK), BF16)],
        in_specs=[SMEM, SMEM] + [VMEM] * (NCOL + 1),
        out_specs=[VMEM, VMEM],
        scratch_shapes=[pltpu.VMEM((W, n), BF16)],
        compiler_params=PARAMS,
    )(col, place, *parts, matrix)


def base_kernel(col, full, matrix, out):
    mine = matrix[:, pl.ds(pl.multiple_of(col[0] * BLK, BLK), BLK)]
    out[...] = jnp.dot(full[...].T, mine, preferred_element_type=F32)


def base_term(col, full, matrix):
    n = full.shape[1]
    return pl.pallas_call(
        base_kernel,
        out_shape=shape((n, BLK), F32),
        in_specs=[SMEM, VMEM, VMEM],
        out_specs=VMEM,
        compiler_params=PARAMS,
    )(col, full, matrix)


def fetch(value):
    column = jnp.stack([take(value, "z", NZ, dz) if dz else value for dz in EVEN])
    even = [take(column, "x", NX, dx) if dx else column for dx in range(NX)]
    near = []
    for group in GROUPS:
        near.append(take(jnp.concatenate([even[dx][0:2] for dx in group]), "z", NZ, 1))
        near.append(take(jnp.concatenate([even[dx][1:3] for dx in group]), "z", NZ, -1))
    return even + near


def back_kernel(count, slots, place, *refs):
    upper, matrix, blocks, own, other, picked, total = refs[:count], *refs[count:]
    for step in range(STEPS):
        for k in range(PER):
            slot = slots[step * PER + k]
            which, where = slot // 16, slot % 16
            for d in range(count):

                @pl.when(which == d)
                def pick():
                    picked[:, k * BLK : (k + 1) * BLK] = upper[d][where]

        rows = slice(step * PER * BLK, (step + 1) * PER * BLK)
        term = jnp.dot(picked[...], blocks[rows, :], preferred_element_type=F32)
        if step == 0:
            total[...] = term
        else:
            total[...] += term
    total[...] = jnp.dot(total[...].astype(BF16), matrix[...], preferred_element_type=F32)
    for i in range(NY):
        start = pl.multiple_of(place[i] * BLK, BLK)
        own[i] = total[:, pl.ds(start, BLK)]
        start = pl.multiple_of(place[NY + i] * BLK, BLK)
        other[i] = total[:, pl.ds(start, BLK)].astype(BF16)


def back(slots, place, upper, matrix, held):
    n = upper[0].shape[1]
    return pl.pallas_call(
        functools.partial(back_kernel, len(upper)),
        out_shape=[shape((NY, n, BLK), F32), shape((NY, n, BLK), BF16)],
        in_specs=[SMEM, SMEM] + [VMEM] * (len(upper) + 2),
        out_specs=[VMEM] * 2,
        scratch_shapes=[pltpu.VMEM((n, PER * BLK), BF16), pltpu.VMEM((n, W), F32)],
        compiler_params=PARAMS,
    )(slots, place, *upper, matrix, held)


def sum_core_kernel(own, other, mine, *outs):
    mine[...] = own[0] + other[0].astype(F32)
    for i in range(1, NY):
        outs[i - 1][...] = (own[i] + other[i].astype(F32)).astype(BF16)


def sum_core(own, other):
    n = own.shape[1]
    return pl.pallas_call(
        sum_core_kernel,
        out_shape=[shape((n, BLK), F32)] + [shape((n, BLK), BF16)] * (NY - 1),
        in_specs=[VMEM] * 2,
        out_specs=[VMEM] * NY,
        compiler_params=PARAMS,
    )(own, other)


def reduce_col(own, other):
    parts = sum_core(own, take(other, "core", NC, 1))
    total = parts[0]
    for d in range(1, NY):
        total = total + give(parts[d], "y", NY, d).astype(F32)
    return total


def body(rhs, dinv, loff, targets):
    levels = rhs.shape[0]
    x, z = lax.axis_index("x"), lax.axis_index("z")
    y, core = lax.axis_index("y"), lax.axis_index("core")
    order = jnp.arange(NY, dtype=jnp.int32)
    rows = (y + order) % NY * NC
    place = jnp.concatenate([rows + core, rows + 1 - core]).astype(jnp.int32)
    col = (y * NC + core).reshape(1).astype(jnp.int32)
    slots = (targets // NZ - x) % NX * NZ + (targets % NZ - z) % NZ
    to_slots, from_slots = look_up(forward_table(), slots), look_up(backward_table(), slots)
    full_d = [None] * levels
    blocks = hold(loff, HOLD)
    bases = []
    incoming = None
    for level in range(levels - 1):
        resid = rhs[level] if level == 0 else rhs[level] - incoming
        parts = gather_col(resid.astype(BF16))
        if level == 0:
            mine = own_rows(place, parts, dinv, blocks[0])
            mine, held = lax.optimization_barrier((mine, dinv))
            for other in list(range(1, levels)) + [0]:
                whole = lax.all_gather(held[other], ("y", "core"), axis=0, tiled=True)
                (full_d[other],) = hold(whole[None], VLIM)
            parts = gather_col(mine)
        outs, full = update(to_slots[level], place, parts, full_d[level] if level else None, blocks[level])
        bases.append(base_term(col, full, full_d[level]))
        if level == 0:
            incoming = route(outs, blocks[0], full_d[1])
        else:
            incoming = route(outs, full_d[2], full_d[0])
    parts = gather_col((rhs[levels - 1] - incoming).astype(BF16))
    solved, solved_bf = top(col, place, parts, full_d[levels - 1])
    result = jnp.zeros(rhs.shape, F32).at[levels - 1].set(solved.T)
    for level in reversed(range(levels - 1)):
        upper = fetch(solved_bf)
        own, other = back(from_slots[level], place, upper, full_d[level], blocks[level])
        solved = bases[level] - reduce_col(own, other)
        solved_bf = solved.astype(BF16)
        result = result.at[level].set(solved.T)
    return result


def solution(mesh):
    grid = Mesh(mesh.devices.reshape(NX, NZ, NY, NC), ("x", "z", "y", "core"))
    split = ("x", "z", "y", "core")
    in_specs = (P(None, split, None), P(None, split, None), P(None, split, None), P(None, split))
    out_specs = P(None, split, None)
    return jax.shard_map(body, mesh=grid, in_specs=in_specs, out_specs=out_specs, check_vma=False)
```

```python
import functools
import jax
import jax.numpy as jnp
from jax import lax
from jax.experimental import pallas as pl
from jax.experimental.pallas import tpu as pltpu
from jax.sharding import Mesh, PartitionSpec as P

BLK = 128
NX, NZ, NY, NC = 4, 8, 4, 2
NCOL = NY * NC
W = NCOL * BLK
OFF = 16
STEPS = 4
PER = OFF // STEPS
F32, BF16 = jnp.float32, jnp.bfloat16
VLIM = 20
SIGN = (-1, -1, 1, 1)
EVEN = (2, 0, 6, 4)
GROUPS = ((0,), (1, 3), (2,))

SMEM = pl.BlockSpec(memory_space=pltpu.SMEM)
VMEM = pl.BlockSpec(memory_space=pltpu.VMEM)
HBM = pl.BlockSpec(memory_space=pltpu.HBM)
PARAMS = pltpu.CompilerParams(vmem_limit_bytes=VLIM * 1024 * 1024)


def shape(dims, dtype):
    return jax.ShapeDtypeStruct(dims, dtype)


def take(value, axis, size, shift):
    return lax.ppermute(value, axis, [(i, (i - shift) % size) for i in range(size)])


def give(value, axis, size, shift):
    return lax.ppermute(value, axis, [(i, (i + shift) % size) for i in range(size)])


def gather_col(value):
    rows = [value] + [take(value, "y", NY, d) for d in range(1, NY)]
    return rows + [take(v, "core", NC, 1) for v in rows]


def fill(place, parts, full):
    for i in range(NCOL):
        start = pl.multiple_of(place[i] * BLK, BLK)
        full[pl.ds(start, BLK), :] = parts[i][...]


def load(source, target, sems, pieces):
    size = target.shape[0] // pieces
    copies = []
    for i in range(pieces):
        rows = pl.ds(i * size, size)
        copies.append(pltpu.make_async_copy(source.at[rows, :], target.at[rows, :], sems.at[i]))
        copies[-1].start()
    return copies


def own_rows_kernel(place, *refs):
    parts, (dinv, out, full, matrix, sem) = refs[:NCOL], refs[NCOL:]
    (copy,) = load(dinv.at[0], matrix, sem, 1)
    fill(place, parts, full)
    copy.wait()
    out[...] = jnp.dot(matrix[...], full[...], preferred_element_type=F32).astype(BF16)


def own_rows(place, parts, dinv):
    n = parts[0].shape[1]
    return pl.pallas_call(
        own_rows_kernel,
        out_shape=shape((BLK, n), BF16),
        in_specs=[SMEM] + [VMEM] * NCOL + [HBM],
        out_specs=VMEM,
        scratch_shapes=[pltpu.VMEM((W, n), BF16), pltpu.VMEM((BLK, W), BF16), pltpu.SemaphoreType.DMA((1,))],
        compiler_params=PARAMS,
    )(place, *parts, dinv)


def forward_table():
    table = [0] * (NX * NZ)
    for dx in range(NX):
        for j, dz in enumerate(EVEN):
            table[dx * NZ + dz] = 2 * dx * 16 + j
            table[dx * NZ + (dz + SIGN[dx]) % NZ] = (2 * dx + 1) * 16 + j
    return table


def backward_table():
    table = [0] * (NX * NZ)
    for g, group in enumerate(GROUPS):
        for i, dx in enumerate(group):
            for j, dz in enumerate(EVEN):
                table[dx * NZ + dz] = dx * 16 + j
            for kind, odd in enumerate(((3, 1), (7, 5))):
                for j, dz in enumerate(odd):
                    table[dx * NZ + dz] = (NX + 2 * g + kind) * 16 + i * 2 + j
    return table


def look_up(table, slots):
    wanted = lax.iota(jnp.int32, len(table))
    values = jnp.array(table, jnp.int32)
    return jnp.sum(jnp.where(slots[..., None] == wanted, values, 0), axis=-1, dtype=jnp.int32)


def update_kernel(level, solve, slots, place, *refs):
    parts, refs = refs[:NCOL], refs[NCOL:]
    if solve:
        inverse, refs = refs[0], refs[1:]
    loff, outs, refs = refs[0], refs[1 : 1 + 2 * NX], refs[1 + 2 * NX :]
    full_out, full, piece, blocks, block_sems = refs[:5]
    if solve:
        matrix, matrix_sem = refs[5:]
        (copy,) = load(inverse, matrix, matrix_sem, 1)
    copies = load(loff.at[level], blocks, block_sems, STEPS)
    for out in outs:
        out[...] = jnp.zeros_like(out)
    fill(place, parts, full)
    if solve:
        copy.wait()
        full[...] = jnp.dot(matrix[...], full[...], preferred_element_type=F32).astype(BF16)
    full_out[...] = full[...]
    for step in range(STEPS):
        copies[step].wait()
        rows = slice(step * PER * BLK, (step + 1) * PER * BLK)
        piece[...] = jnp.dot(blocks[rows, :], full[...], preferred_element_type=F32).astype(BF16)
        for k in range(PER):
            slot = slots[step * PER + k]
            which, where = slot // 16, slot % 16
            for d in range(2 * NX):

                @pl.when(which == d)
                def put():
                    outs[d][where] = piece[k * BLK : (k + 1) * BLK, :]


def update(level, slots, place, parts, matrix, loff):
    n = parts[0].shape[1]
    solve = matrix is not None
    args = [slots, place, *parts] + ([matrix] if solve else []) + [loff]
    scratch = [
        pltpu.VMEM((W, n), BF16),
        pltpu.VMEM((PER * BLK, n), BF16),
        pltpu.VMEM((OFF * BLK, W), BF16),
        pltpu.SemaphoreType.DMA((STEPS,)),
    ]
    if solve:
        scratch += [pltpu.VMEM((W, W), BF16), pltpu.SemaphoreType.DMA((1,))]
    *outs, full = pl.pallas_call(
        functools.partial(update_kernel, level, solve),
        out_shape=[shape((4, BLK, n), BF16)] * (2 * NX) + [shape((W, n), BF16)],
        in_specs=[SMEM, SMEM] + [VMEM] * NCOL + [HBM] * (1 + solve),
        out_specs=[VMEM] * (2 * NX + 1),
        scratch_shapes=scratch,
        compiler_params=PARAMS,
    )(*args)
    return outs, full


def sum_near_kernel(even, near, out):
    for j in range(4):
        out[j] = (even[j].astype(F32) + near[j].astype(F32)).astype(BF16)


def sum_near(even, near):
    return pl.pallas_call(
        sum_near_kernel,
        out_shape=shape(even.shape, BF16),
        in_specs=[VMEM] * 2,
        out_specs=VMEM,
        compiler_params=PARAMS,
    )(even, near)


def sum_x_kernel(*refs):
    ins, outs = refs[: NX + 1], refs[NX + 1 :]
    for j in range(4):
        total = ins[0][j].astype(F32)
        for other in ins[1:]:
            total += other[j].astype(F32)
        outs[j][...] = total.astype(outs[j].dtype)


def sum_x(ins):
    n = ins[0].shape[2]
    return pl.pallas_call(
        sum_x_kernel,
        out_shape=[shape((BLK, n), BF16 if dz else F32) for dz in EVEN],
        in_specs=[VMEM] * (NX + 1),
        out_specs=[VMEM] * 4,
        compiler_params=PARAMS,
    )(*ins)


def route(outs):
    near = {dx: give(outs[2 * dx + 1], "z", NZ, SIGN[dx]) for dx in (2, 1, 3, 0)}
    got = [outs[0], near[0]]
    for dx in (2, 1, 3):
        got.append(give(sum_near(outs[2 * dx], near[dx]), "x", NX, dx))
    parts = sum_x(got)
    total = parts[EVEN.index(0)]
    for j, dz in enumerate(EVEN):
        if dz:
            total = total + give(parts[j], "z", NZ, dz).astype(F32)
    return total


def top_kernel(col, place, *refs):
    parts, (inverse, out, out_bf, full, matrix, sem) = refs[:NCOL], refs[NCOL:]
    (copy,) = load(inverse, matrix, sem, 1)
    fill(place, parts, full)
    copy.wait()
    forward = jnp.dot(matrix[...], full[...], preferred_element_type=F32)
    mine = matrix[:, pl.ds(pl.multiple_of(col[0] * BLK, BLK), BLK)]
    solved = jnp.dot(forward.T.astype(BF16), mine, preferred_element_type=F32)
    out[...] = solved
    out_bf[...] = solved.astype(BF16)


def top(col, place, parts, matrix):
    n = parts[0].shape[1]
    return pl.pallas_call(
        top_kernel,
        out_shape=[shape((n, BLK), F32), shape((n, BLK), BF16)],
        in_specs=[SMEM, SMEM] + [VMEM] * NCOL + [HBM],
        out_specs=[VMEM, VMEM],
        scratch_shapes=[pltpu.VMEM((W, n), BF16), pltpu.VMEM((W, W), BF16), pltpu.SemaphoreType.DMA((1,))],
        compiler_params=PARAMS,
    )(col, place, *parts, matrix)


def base_kernel(col, full, inverse, out, mine, sem):
    columns = pl.ds(pl.multiple_of(col[0] * BLK, BLK), BLK)
    copy = pltpu.make_async_copy(inverse.at[:, columns], mine, sem.at[0])
    copy.start()
    turned = full[...].T
    copy.wait()
    out[...] = jnp.dot(turned, mine[...], preferred_element_type=F32)


def base_term(col, full, matrix):
    n = full.shape[1]
    return pl.pallas_call(
        base_kernel,
        out_shape=shape((n, BLK), F32),
        in_specs=[SMEM, VMEM, HBM],
        out_specs=VMEM,
        scratch_shapes=[pltpu.VMEM((W, BLK), BF16), pltpu.SemaphoreType.DMA((1,))],
        compiler_params=PARAMS,
    )(col, full, matrix)


def fetch(value):
    column = jnp.stack([take(value, "z", NZ, dz) if dz else value for dz in EVEN])
    even = [take(column, "x", NX, dx) if dx else column for dx in range(NX)]
    near = []
    for group in GROUPS:
        near.append(take(jnp.concatenate([even[dx][0:2] for dx in group]), "z", NZ, 1))
        near.append(take(jnp.concatenate([even[dx][1:3] for dx in group]), "z", NZ, -1))
    return even + near


def back_kernel(level, count, slots, place, *refs):
    upper, (inverse, loff, own, other, picked, total) = refs[:count], refs[count : count + 6]
    blocks, block_sems, matrix, matrix_sem = refs[count + 6 :]
    copies = load(loff.at[level], blocks, block_sems, STEPS)
    (copy,) = load(inverse, matrix, matrix_sem, 1)
    for step in range(STEPS):
        for k in range(PER):
            slot = slots[step * PER + k]
            which, where = slot // 16, slot % 16
            for d in range(count):

                @pl.when(which == d)
                def pick():
                    picked[:, k * BLK : (k + 1) * BLK] = upper[d][where]

        rows = slice(step * PER * BLK, (step + 1) * PER * BLK)
        copies[step].wait()
        term = jnp.dot(picked[...], blocks[rows, :], preferred_element_type=F32)
        if step == 0:
            total[...] = term
        else:
            total[...] += term
    copy.wait()
    total[...] = jnp.dot(total[...].astype(BF16), matrix[...], preferred_element_type=F32)
    for i in range(NY):
        start = pl.multiple_of(place[i] * BLK, BLK)
        own[i] = total[:, pl.ds(start, BLK)]
        start = pl.multiple_of(place[NY + i] * BLK, BLK)
        other[i] = total[:, pl.ds(start, BLK)].astype(BF16)


def back(level, slots, place, upper, matrix, loff):
    n = upper[0].shape[1]
    return pl.pallas_call(
        functools.partial(back_kernel, level, len(upper)),
        out_shape=[shape((NY, n, BLK), F32), shape((NY, n, BLK), BF16)],
        in_specs=[SMEM, SMEM] + [VMEM] * len(upper) + [HBM] * 2,
        out_specs=[VMEM] * 2,
        scratch_shapes=[
            pltpu.VMEM((n, PER * BLK), BF16),
            pltpu.VMEM((n, W), F32),
            pltpu.VMEM((OFF * BLK, W), BF16),
            pltpu.SemaphoreType.DMA((STEPS,)),
            pltpu.VMEM((W, W), BF16),
            pltpu.SemaphoreType.DMA((1,)),
        ],
        compiler_params=PARAMS,
    )(slots, place, *upper, matrix, loff)


def sum_core_kernel(own, other, mine, *outs):
    mine[...] = own[0] + other[0].astype(F32)
    for i in range(1, NY):
        outs[i - 1][...] = (own[i] + other[i].astype(F32)).astype(BF16)


def sum_core(own, other):
    n = own.shape[1]
    return pl.pallas_call(
        sum_core_kernel,
        out_shape=[shape((n, BLK), F32)] + [shape((n, BLK), BF16)] * (NY - 1),
        in_specs=[VMEM] * 2,
        out_specs=[VMEM] * NY,
        compiler_params=PARAMS,
    )(own, other)


def reduce_col(own, other):
    parts = sum_core(own, take(other, "core", NC, 1))
    total = parts[0]
    for d in range(1, NY):
        total = total + give(parts[d], "y", NY, d).astype(F32)
    return total


def body(rhs, dinv, loff, targets):
    levels = rhs.shape[0]
    x, z = lax.axis_index("x"), lax.axis_index("z")
    y, core = lax.axis_index("y"), lax.axis_index("core")
    loff = pltpu.with_memory_space_constraint(loff, pltpu.HBM)
    order = jnp.arange(NY, dtype=jnp.int32)
    rows = (y + order) % NY * NC
    place = jnp.concatenate([rows + core, rows + 1 - core]).astype(jnp.int32)
    col = (y * NC + core).reshape(1).astype(jnp.int32)
    slots = (targets // NZ - x) % NX * NZ + (targets % NZ - z) % NZ
    to_slots, from_slots = look_up(forward_table(), slots), look_up(backward_table(), slots)
    full_d = [None] * levels
    bases = []
    incoming = None
    for level in range(levels - 1):
        resid = rhs[level] if level == 0 else rhs[level] - incoming
        parts = gather_col(resid.astype(BF16))
        if level == 0:
            mine = own_rows(place, parts, dinv)
            mine, held = lax.optimization_barrier((mine, dinv))
            for other in list(range(1, levels)) + [0]:
                whole = lax.all_gather(held[other], ("y", "core"), axis=0, tiled=True)
                full_d[other] = pltpu.with_memory_space_constraint(whole, pltpu.HBM)
            parts = gather_col(mine)
        outs, full = update(level, to_slots[level], place, parts, full_d[level] if level else None, loff)
        bases.append(base_term(col, full, full_d[level]))
        incoming = route(outs)
    parts = gather_col((rhs[levels - 1] - incoming).astype(BF16))
    solved, solved_bf = top(col, place, parts, full_d[levels - 1])
    result = jnp.zeros(rhs.shape, F32).at[levels - 1].set(solved.T)
    for level in reversed(range(levels - 1)):
        upper = fetch(solved_bf)
        own, other = back(level, from_slots[level], place, upper, full_d[level], loff)
        solved = bases[level] - reduce_col(own, other)
        solved_bf = solved.astype(BF16)
        result = result.at[level].set(solved.T)
    return result


def solution(mesh):
    grid = Mesh(mesh.devices.reshape(NX, NZ, NY, NC), ("x", "z", "y", "core"))
    split = ("x", "z", "y", "core")
    in_specs = (P(None, split, None), P(None, split, None), P(None, split, None), P(None, split))
    out_specs = P(None, split, None)
    return jax.shard_map(body, mesh=grid, in_specs=in_specs, out_specs=out_specs, check_vma=False)
```

```python
import functools
import jax
import jax.numpy as jnp
from jax import lax
from jax.experimental import pallas as pl
from jax.experimental.pallas import tpu as pltpu
from jax.sharding import Mesh, PartitionSpec as P

BLK = 128
NX, NZ, NY, NC = 4, 8, 4, 2
NCOL = NY * NC
W = NCOL * BLK
OFF = 16
STEPS = 4
PER = OFF // STEPS
F32, BF16 = jnp.float32, jnp.bfloat16
VLIM = 20
SIGN = (-1, -1, 1, 1)
EVEN = (2, 0, 6, 4)
GROUPS = ((0,), (1, 3), (2,))

SMEM = pl.BlockSpec(memory_space=pltpu.SMEM)
VMEM = pl.BlockSpec(memory_space=pltpu.VMEM)
HBM = pl.BlockSpec(memory_space=pltpu.HBM)
PARAMS = pltpu.CompilerParams(vmem_limit_bytes=VLIM * 1024 * 1024)


def shape(dims, dtype):
    return jax.ShapeDtypeStruct(dims, dtype)


def take(value, axis, size, shift):
    return lax.ppermute(value, axis, [(i, (i - shift) % size) for i in range(size)])


def give(value, axis, size, shift):
    return lax.ppermute(value, axis, [(i, (i + shift) % size) for i in range(size)])


def gather_col(value):
    rows = [value] + [take(value, "y", NY, d) for d in range(1, NY)]
    return rows + [take(v, "core", NC, 1) for v in rows]


def fill(place, parts, full):
    for i in range(NCOL):
        start = pl.multiple_of(place[i] * BLK, BLK)
        full[pl.ds(start, BLK), :] = parts[i][...]


def piece_of(source, target, sems, i, pieces):
    size = target.shape[0] // pieces
    rows = pl.ds(pl.multiple_of(i * size, size), size)
    return pltpu.make_async_copy(source.at[rows, :], target.at[rows, :], sems.at[i])


def load(source, target, sems, pieces):
    copies = [piece_of(source, target, sems, i, pieces) for i in range(pieces)]
    for copy in copies:
        copy.start()
    return copies


def own_rows_kernel(place, *refs):
    parts, (dinv, out, full, matrix, sem) = refs[:NCOL], refs[NCOL:]
    (copy,) = load(dinv.at[0], matrix, sem, 1)
    fill(place, parts, full)
    copy.wait()
    out[...] = jnp.dot(matrix[...], full[...], preferred_element_type=F32).astype(BF16)


def own_rows(place, parts, dinv):
    n = parts[0].shape[1]
    return pl.pallas_call(
        own_rows_kernel,
        out_shape=shape((BLK, n), BF16),
        in_specs=[SMEM] + [VMEM] * NCOL + [HBM],
        out_specs=VMEM,
        scratch_shapes=[pltpu.VMEM((W, n), BF16), pltpu.VMEM((BLK, W), BF16), pltpu.SemaphoreType.DMA((1,))],
        compiler_params=PARAMS,
    )(place, *parts, dinv)


def forward_table():
    table = [0] * (NX * NZ)
    for dx in range(NX):
        for j, dz in enumerate(EVEN):
            table[dx * NZ + dz] = 2 * dx * 4 + j
            table[dx * NZ + (dz + SIGN[dx]) % NZ] = (2 * dx + 1) * 4 + j
    return table


def backward_table():
    table = [0] * (NX * NZ)
    start = NX * 4
    for dx in range(NX):
        for j, dz in enumerate(EVEN):
            table[dx * NZ + dz] = dx * 4 + j
    for group in GROUPS:
        for odd in ((3, 1), (7, 5)):
            for dx in group:
                for dz in odd:
                    table[dx * NZ + dz] = start
                    start += 1
    return table


def look_up(table, slots):
    wanted = lax.iota(jnp.int32, len(table))
    values = jnp.array(table, jnp.int32)
    return jnp.sum(jnp.where(slots[..., None] == wanted, values, 0), axis=-1, dtype=jnp.int32)


def update_kernel(level, solve, slots, place, *refs):
    parts, refs = refs[:NCOL], refs[NCOL:]
    if solve:
        inverse, refs = refs[0], refs[1:]
    loff, outs, refs = refs[0], refs[1 : 1 + 2 * NX], refs[1 + 2 * NX :]
    full_out, full, placed, blocks, block_sems = refs[:5]
    if solve:
        matrix, matrix_sem = refs[5:]
        (copy,) = load(inverse, matrix, matrix_sem, 1)
    else:
        load(loff.at[level], blocks, block_sems, STEPS)
    fill(place, parts, full)
    placed[...] = jnp.zeros_like(placed)
    if solve:
        copy.wait()
        load(loff.at[level], blocks, block_sems, STEPS)
        full[...] = jnp.dot(matrix[...], full[...], preferred_element_type=F32).astype(BF16)
    full_out[...] = full[...]

    def advance(step, carry):
        piece_of(loff.at[level], blocks, block_sems, step, STEPS).wait()
        rows = pl.ds(pl.multiple_of(step * PER * BLK, PER * BLK), PER * BLK)
        terms = jnp.dot(blocks[rows, :], full[...], preferred_element_type=F32).astype(BF16)
        for k in range(PER):
            placed[slots[step * PER + k]] = terms[k * BLK : (k + 1) * BLK, :]
        return carry

    lax.fori_loop(0, STEPS, advance, 0)
    for d in range(2 * NX):
        outs[d][...] = placed[4 * d : 4 * d + 4]


def update(level, slots, place, parts, matrix, loff):
    n = parts[0].shape[1]
    solve = matrix is not None
    args = [slots, place, *parts] + ([matrix] if solve else []) + [loff]
    scratch = [
        pltpu.VMEM((W, n), BF16),
        pltpu.VMEM((NX * NZ, BLK, n), BF16),
        pltpu.VMEM((OFF * BLK, W), BF16),
        pltpu.SemaphoreType.DMA((STEPS,)),
    ]
    if solve:
        scratch += [pltpu.VMEM((W, W), BF16), pltpu.SemaphoreType.DMA((1,))]
    *outs, full = pl.pallas_call(
        functools.partial(update_kernel, level, solve),
        out_shape=[shape((4, BLK, n), BF16)] * (2 * NX) + [shape((W, n), BF16)],
        in_specs=[SMEM, SMEM] + [VMEM] * NCOL + [HBM] * (1 + solve),
        out_specs=[VMEM] * (2 * NX + 1),
        scratch_shapes=scratch,
        compiler_params=PARAMS,
    )(*args)
    return outs, full


def sum_near_kernel(even, near, out):
    for j in range(4):
        out[j] = (even[j].astype(F32) + near[j].astype(F32)).astype(BF16)


def sum_near(even, near):
    return pl.pallas_call(
        sum_near_kernel,
        out_shape=shape(even.shape, BF16),
        in_specs=[VMEM] * 2,
        out_specs=VMEM,
        compiler_params=PARAMS,
    )(even, near)


def sum_x_kernel(*refs):
    ins, outs = refs[: NX + 1], refs[NX + 1 :]
    for j in range(4):
        total = ins[0][j].astype(F32)
        for other in ins[1:]:
            total += other[j].astype(F32)
        outs[j][...] = total.astype(outs[j].dtype)


def sum_x(ins):
    n = ins[0].shape[2]
    return pl.pallas_call(
        sum_x_kernel,
        out_shape=[shape((BLK, n), BF16 if dz else F32) for dz in EVEN],
        in_specs=[VMEM] * (NX + 1),
        out_specs=[VMEM] * 4,
        compiler_params=PARAMS,
    )(*ins)


def route(outs):
    near = {dx: give(outs[2 * dx + 1], "z", NZ, SIGN[dx]) for dx in (2, 1, 3, 0)}
    got = [outs[0], near[0]]
    for dx in (2, 1, 3):
        got.append(give(sum_near(outs[2 * dx], near[dx]), "x", NX, dx))
    parts = sum_x(got)
    total = parts[EVEN.index(0)]
    for j, dz in enumerate(EVEN):
        if dz:
            total = total + give(parts[j], "z", NZ, dz).astype(F32)
    return total


def top_kernel(col, place, *refs):
    parts, (inverse, out, out_bf, full, matrix, sem) = refs[:NCOL], refs[NCOL:]
    (copy,) = load(inverse, matrix, sem, 1)
    fill(place, parts, full)
    copy.wait()
    forward = jnp.dot(matrix[...], full[...], preferred_element_type=F32)
    mine = matrix[:, pl.ds(pl.multiple_of(col[0] * BLK, BLK), BLK)]
    solved = jnp.dot(forward.T.astype(BF16), mine, preferred_element_type=F32)
    out[...] = solved
    out_bf[...] = solved.astype(BF16)


def top(col, place, parts, matrix):
    n = parts[0].shape[1]
    return pl.pallas_call(
        top_kernel,
        out_shape=[shape((n, BLK), F32), shape((n, BLK), BF16)],
        in_specs=[SMEM, SMEM] + [VMEM] * NCOL + [HBM],
        out_specs=[VMEM, VMEM],
        scratch_shapes=[pltpu.VMEM((W, n), BF16), pltpu.VMEM((W, W), BF16), pltpu.SemaphoreType.DMA((1,))],
        compiler_params=PARAMS,
    )(col, place, *parts, matrix)


def base_kernel(col, full, inverse, out, mine, sem):
    columns = pl.ds(pl.multiple_of(col[0] * BLK, BLK), BLK)
    copy = pltpu.make_async_copy(inverse.at[:, columns], mine, sem.at[0])
    copy.start()
    turned = full[...].T
    copy.wait()
    out[...] = jnp.dot(turned, mine[...], preferred_element_type=F32)


def base_term(col, full, matrix):
    n = full.shape[1]
    return pl.pallas_call(
        base_kernel,
        out_shape=shape((n, BLK), F32),
        in_specs=[SMEM, VMEM, HBM],
        out_specs=VMEM,
        scratch_shapes=[pltpu.VMEM((W, BLK), BF16), pltpu.SemaphoreType.DMA((1,))],
        compiler_params=PARAMS,
    )(col, full, matrix)


def fetch(value):
    column = jnp.stack([take(value, "z", NZ, dz) if dz else value for dz in EVEN])
    even = [take(column, "x", NX, dx) if dx else column for dx in range(NX)]
    near = []
    for group in GROUPS:
        near.append(take(jnp.concatenate([even[dx][0:2] for dx in group]), "z", NZ, 1))
        near.append(take(jnp.concatenate([even[dx][1:3] for dx in group]), "z", NZ, -1))
    return even + near


def back_kernel(level, count, slots, place, *refs):
    upper, (inverse, loff, own, other, picked, total) = refs[:count], refs[count : count + 6]
    row, blocks, block_sems, matrix, matrix_sem = refs[count + 6 :]
    load(loff.at[level], blocks, block_sems, STEPS)
    (copy,) = load(inverse, matrix, matrix_sem, 1)
    start = 0
    for part in upper:
        row[start : start + part.shape[0]] = part[...]
        start += part.shape[0]
    total[...] = jnp.zeros_like(total)

    def advance(step, carry):
        for k in range(PER):
            picked[:, k * BLK : (k + 1) * BLK] = row[slots[step * PER + k]]
        piece_of(loff.at[level], blocks, block_sems, step, STEPS).wait()
        rows = pl.ds(pl.multiple_of(step * PER * BLK, PER * BLK), PER * BLK)
        total[...] += jnp.dot(picked[...], blocks[rows, :], preferred_element_type=F32)
        return carry

    lax.fori_loop(0, STEPS, advance, 0)
    copy.wait()
    total[...] = jnp.dot(total[...].astype(BF16), matrix[...], preferred_element_type=F32)
    for i in range(NY):
        start = pl.multiple_of(place[i] * BLK, BLK)
        own[i] = total[:, pl.ds(start, BLK)]
        start = pl.multiple_of(place[NY + i] * BLK, BLK)
        other[i] = total[:, pl.ds(start, BLK)].astype(BF16)


def back(level, slots, place, upper, matrix, loff):
    n = upper[0].shape[1]
    return pl.pallas_call(
        functools.partial(back_kernel, level, len(upper)),
        out_shape=[shape((NY, n, BLK), F32), shape((NY, n, BLK), BF16)],
        in_specs=[SMEM, SMEM] + [VMEM] * len(upper) + [HBM] * 2,
        out_specs=[VMEM] * 2,
        scratch_shapes=[
            pltpu.VMEM((n, PER * BLK), BF16),
            pltpu.VMEM((n, W), F32),
            pltpu.VMEM((NX * NZ, n, BLK), BF16),
            pltpu.VMEM((OFF * BLK, W), BF16),
            pltpu.SemaphoreType.DMA((STEPS,)),
            pltpu.VMEM((W, W), BF16),
            pltpu.SemaphoreType.DMA((1,)),
        ],
        compiler_params=PARAMS,
    )(slots, place, *upper, matrix, loff)


def sum_core_kernel(own, other, mine, *outs):
    mine[...] = own[0] + other[0].astype(F32)
    for i in range(1, NY):
        outs[i - 1][...] = (own[i] + other[i].astype(F32)).astype(BF16)


def sum_core(own, other):
    n = own.shape[1]
    return pl.pallas_call(
        sum_core_kernel,
        out_shape=[shape((n, BLK), F32)] + [shape((n, BLK), BF16)] * (NY - 1),
        in_specs=[VMEM] * 2,
        out_specs=[VMEM] * NY,
        compiler_params=PARAMS,
    )(own, other)


def reduce_col(own, other):
    parts = sum_core(own, take(other, "core", NC, 1))
    total = parts[0]
    for d in range(1, NY):
        total = total + give(parts[d], "y", NY, d).astype(F32)
    return total


def body(rhs, dinv, loff, targets):
    levels = rhs.shape[0]
    x, z = lax.axis_index("x"), lax.axis_index("z")
    y, core = lax.axis_index("y"), lax.axis_index("core")
    loff = pltpu.with_memory_space_constraint(loff, pltpu.HBM)
    order = jnp.arange(NY, dtype=jnp.int32)
    rows = (y + order) % NY * NC
    place = jnp.concatenate([rows + core, rows + 1 - core]).astype(jnp.int32)
    col = (y * NC + core).reshape(1).astype(jnp.int32)
    slots = (targets // NZ - x) % NX * NZ + (targets % NZ - z) % NZ
    to_slots, from_slots = look_up(forward_table(), slots), look_up(backward_table(), slots)
    full_d = [None] * levels
    bases = []
    incoming = None
    for level in range(levels - 1):
        resid = rhs[level] if level == 0 else rhs[level] - incoming
        parts = gather_col(resid.astype(BF16))
        if level == 0:
            mine = own_rows(place, parts, dinv)
            mine, held = lax.optimization_barrier((mine, dinv))
            for other in list(range(1, levels)) + [0]:
                whole = lax.all_gather(held[other], ("y", "core"), axis=0, tiled=True)
                full_d[other] = pltpu.with_memory_space_constraint(whole, pltpu.HBM)
            parts = gather_col(mine)
        outs, full = update(level, to_slots[level], place, parts, full_d[level] if level else None, loff)
        bases.append(base_term(col, full, full_d[level]))
        incoming = route(outs)
    parts = gather_col((rhs[levels - 1] - incoming).astype(BF16))
    solved, solved_bf = top(col, place, parts, full_d[levels - 1])
    result = jnp.zeros(rhs.shape, F32).at[levels - 1].set(solved.T)
    for level in reversed(range(levels - 1)):
        upper = fetch(solved_bf)
        own, other = back(level, from_slots[level], place, upper, full_d[level], loff)
        solved = bases[level] - reduce_col(own, other)
        solved_bf = solved.astype(BF16)
        result = result.at[level].set(solved.T)
    return result


def solution(mesh):
    grid = Mesh(mesh.devices.reshape(NX, NZ, NY, NC), ("x", "z", "y", "core"))
    split = ("x", "z", "y", "core")
    in_specs = (P(None, split, None), P(None, split, None), P(None, split, None), P(None, split))
    out_specs = P(None, split, None)
    return jax.shard_map(body, mesh=grid, in_specs=in_specs, out_specs=out_specs, check_vma=False)
```
